32 devices in a mesh: row: 8 (over y, x, core), col: 4 (over z).
Axes of the slice: x: 2, y: 2, z: 4, core: 2. Of those that a mesh axis runs over, the one named last changes fastest.
Arguments:
- panel: float32 [6144, 256], P('row', 'col'), may hold values from -6 to 6
- trailing: float32 [6144, 12032], P('row', 'col'), may hold values from -6 to 6
Outputs:
- projections: float32 [12032, 256], P('col')
- remainder: float32 [6144, 12032], P('row', 'col')
The draws below stay inside these ranges and needn't reach their ends.
All inputs are finite; a program needn't handle non-finite values.
Results may differ from the reference program's by a relative error of at most 0.000075.
Values sent between devices are 32-bit elements; how exact they have to be, the bound alone decides.
No kernel may reach another device: no remote copies, remote signals or barrier semaphores. Data moves between devices by JAX's collectives and lax.ppermute only.
A program may use at most 64 MiB of HBM per device.

```python
import jax
import jax.numpy as jnp
from jax import lax

B = 256
TRAIL = 12032
ROWS = 6144


def levels(own_key, dims, split, smallest, high):
    def one(axis_at, blocks):
        steps = jax.random.uniform(jax.random.fold_in(jax.random.fold_in(own_key, 6), axis_at), (blocks,), jnp.float32, smallest / len(split), high / len(split))
        return jnp.repeat(jnp.exp(steps), dims[axis_at] // blocks).reshape((-1,) + (1,) * (len(dims) - axis_at - 1))

    loudness = one(*split[0])
    for cut in split[1:]:
        loudness = loudness * one(*cut)
    return loudness


def gaussian(rng, dims, deviation, limit, cuts=(), kind=jnp.bfloat16):
    array = deviation * jax.random.normal(rng, dims, jnp.float32)
    if cuts:
        array = array * levels(rng, dims, cuts, -0.22, 0.18)
    return jnp.clip(array, -limit, limit).astype(kind)


def setup_inputs(seed: int = 0) -> dict:
    keys = jax.random.split(jax.random.key(seed), 3)
    return {
        "panel": gaussian(keys[0], (ROWS, B), 1.0, 6.0, ((0, 8), (1, 4)), jnp.float32),
        "trailing": gaussian(keys[1], (ROWS, TRAIL), 1.0, 6.0, ((0, 8), (1, 4)), jnp.float32),
    }


def reference(panel, trailing):
    highest = lax.Precision.HIGHEST
    panel_gram = jnp.dot(panel.T.astype(jnp.float32), panel.astype(jnp.float32), precision=highest, preferred_element_type=jnp.float32)
    lower_factor = jnp.linalg.cholesky(panel_gram)
    orthonormal = jax.scipy.linalg.solve_triangular(lower_factor, panel.T, lower=True).T
    cross_terms = jnp.dot(trailing.T.astype(jnp.float32), panel.astype(jnp.float32), precision=highest, preferred_element_type=jnp.float32)
    projections = jax.scipy.linalg.solve_triangular(lower_factor, cross_terms.T, lower=True).T
    remainder = trailing - jnp.dot(orthonormal.astype(jnp.float32), projections.T.astype(jnp.float32), precision=highest, preferred_element_type=jnp.float32)
    return (projections, remainder)
```

```python
import functools

import jax
import jax.numpy as jnp
from jax import lax
from jax.experimental import pallas as pl
from jax.experimental.pallas import tpu as pltpu
from jax.sharding import PartitionSpec as P

F32, BF16 = jnp.float32, jnp.bfloat16
HIGHEST = lax.Precision.HIGHEST
NT, NN, TN = ((1,), (1,)), ((1,), (0,)), ((0,), (0,))
LANES, NB = 128, 64
VMEM_LIMIT = 40 * 2**20


def dot(a, b, dims, precision=None):
    return lax.dot_general(a, b, (dims, ((), ())), precision=precision, preferred_element_type=F32)


def split(x):
    hi = x.astype(BF16)
    return hi, (x - hi.astype(F32)).astype(BF16)


def params():
    return pltpu.CompilerParams(vmem_limit_bytes=VMEM_LIMIT)


def cost(flops, bytes_accessed):
    return pl.CostEstimate(flops=flops, bytes_accessed=bytes_accessed, transcendentals=0)


def block_rows(m):
    for b in (752, 376):
        if m % b == 0:
            return b
    return m


def cross_kernel(p_ref, t_ref, c_ref):
    n = p_ref.shape[0]
    p_hi, p_lo = split(p_ref[...])
    t_hi, t_lo = split(t_ref[...])
    both = dot(t_hi, jnp.concatenate([p_hi, p_lo], axis=0), NT)
    c_ref[...] = both[:, :n] + both[:, n:] + dot(t_lo, p_hi, NT)


def cross(p_t, t_t):
    n, k = p_t.shape
    m = t_t.shape[0]
    b = block_rows(m)
    return pl.pallas_call(
        cross_kernel,
        grid=(m // b,),
        in_specs=[pl.BlockSpec((n, k), lambda i: (0, 0)), pl.BlockSpec((b, k), lambda i: (i, 0))],
        out_specs=pl.BlockSpec((b, n), lambda i: (i, 0)),
        out_shape=jax.ShapeDtypeStruct((m, n), F32),
        compiler_params=params(),
        cost_estimate=cost(6 * n * k * m, 4 * (k * m + n * m + n * k)),
        name="cross",
    )(p_t, t_t)


def gram_kernel(p_ref, g_ref):
    p = p_ref[...]
    g_ref[...] = dot(p, p, NT, HIGHEST)


def gram(p_t):
    n, k = p_t.shape
    return pl.pallas_call(
        gram_kernel,
        out_shape=jax.ShapeDtypeStruct((n, n), F32),
        in_specs=[pl.BlockSpec(memory_space=pltpu.VMEM)],
        out_specs=pl.BlockSpec(memory_space=pltpu.VMEM),
        compiler_params=params(),
        cost_estimate=cost(12 * n * n * k, 4 * (n * k + n * n)),
        name="gram",
    )(p_t)


def tile(x):
    return jnp.broadcast_to(x, (8, LANES))


def eliminate(rows):
    sub = lax.broadcasted_iota(jnp.int32, (8, LANES), 0)
    n = len(rows)
    scaled = []
    for g in range(n):
        cols = [[tile(rows[i][:, 8 * g + c : 8 * g + c + 1]) for i in range(g, n)] for c in range(8)]
        own = rows[g]
        pivots = jnp.ones((8, LANES), F32)
        factors, lines = [], []
        for c in range(8):
            pivot = tile(cols[c][0][c : c + 1, :])
            inv = 1.0 / pivot
            f = [x * inv for x in cols[c]]
            f[0] = jnp.where(sub > c, f[0], 0.0)
            pivots = jnp.where(sub == c, pivot, pivots)
            for later in range(c + 1, 8):
                e = tile(cols[later][0][c : c + 1, :])
                cols[later] = [x - y * e for x, y in zip(cols[later], f)]
            line = tile(own[c : c + 1, :])
            own = own - f[0] * line
            factors.append(f)
            lines.append(line)
        for i in range(g + 1, n):
            for c in range(8):
                rows[i] = rows[i] - factors[c][i - g] * lines[c]
        scaled.append(own * lax.rsqrt(pivots))
    return scaled


def factor_kernel(g_ref, p_ref, lh_ref, ll_ref, qh_ref, ql_ref, work, linv):
    n = g_ref.shape[0]
    work[:, :n] = g_ref[...]
    i0 = lax.broadcasted_iota(jnp.int32, (n, n), 0)
    i1 = lax.broadcasted_iota(jnp.int32, (n, n), 1)
    eye = (i0 == i1).astype(F32)
    work[:, n:] = eye
    for s in range(0, n, NB):
        augmented = jnp.concatenate([work[s : s + NB, s : s + NB], eye[:NB, :NB]], axis=1)
        rows = eliminate([augmented[8 * i : 8 * i + 8] for i in range(NB // 8)])
        inv = jnp.concatenate(rows, axis=0)[:, NB:]
        r = dot(inv, work[s : s + NB, :], NN, HIGHEST)
        linv[s : s + NB, :] = r[:, n:]
        if s + NB < n:
            work[s + NB :, :] -= dot(r[:, s + NB : n], r, TN, HIGHEST)
    lh_ref[...], ll_ref[...] = split(linv[...])
    qh_ref[...], ql_ref[...] = split(dot(linv[...], p_ref[...], NN, HIGHEST))


def factor(g, p_t):
    n, k = p_t.shape
    vm = pl.BlockSpec(memory_space=pltpu.VMEM)
    return pl.pallas_call(
        factor_kernel,
        out_shape=[jax.ShapeDtypeStruct((n, n), BF16)] * 2 + [jax.ShapeDtypeStruct((n, k), BF16)] * 2,
        in_specs=[vm] * 2,
        out_specs=[vm] * 4,
        scratch_shapes=[pltpu.VMEM((n, 2 * n), F32), pltpu.VMEM((n, n), F32)],
        compiler_params=params(),
        cost_estimate=cost(10**10, 10**6),
        name="factor",
    )(g, p_t)


def update_kernel(first_ref, lh_ref, ll_ref, qh_ref, ql_ref, ca_ref, cb_ref, t_ref, p_ref, r_ref):
    a, b = ca_ref[...], cb_ref[...]
    swap = first_ref[0] != 0
    c_hi, c_lo = split(jnp.concatenate([jnp.where(swap, b, a), jnp.where(swap, a, b)], axis=1))
    lh, ll, qh, ql = lh_ref[...], ll_ref[...], qh_ref[...], ql_ref[...]
    p = dot(c_hi, lh, NT) + dot(c_lo, lh, NT) + dot(c_hi, ll, NT)
    p_ref[...] = p
    p_hi, p_lo = split(p)
    r_ref[...] = t_ref[...] - (dot(p_hi, qh, NN) + dot(p_lo, qh, NN) + dot(p_hi, ql, NN))


def update(first, lh, ll, qh, ql, ca, cb, t_t):
    n, k = qh.shape
    m = t_t.shape[0]
    b = block_rows(m)
    whole = lambda shape: pl.BlockSpec(shape, lambda i: (0, 0))
    part = lambda width: pl.BlockSpec((b, width), lambda i: (i, 0))
    return pl.pallas_call(
        update_kernel,
        grid=(m // b,),
        in_specs=[pl.BlockSpec(memory_space=pltpu.SMEM), whole((n, n)), whole((n, n)), whole((n, k)), whole((n, k)),
                  part(n // 2), part(n // 2), part(k)],
        out_specs=[part(n), part(k)],
        out_shape=[jax.ShapeDtypeStruct((m, n), F32), jax.ShapeDtypeStruct((m, k), F32)],
        compiler_params=params(),
        cost_estimate=cost(6 * n * (n + k) * m, 4 * m * (2 * k + 2 * n)),
        name="update",
    )(first, lh, ll, qh, ql, ca, cb, t_t)


class Rows:
    def __init__(self, count):
        self.count = count
        self.me = lax.axis_index("row")
        bits = list(range(1, count.bit_length() - 1))
        self.stages = [(0, 0)] + list(zip(bits, bits[::-1]))

    def swap(self, x, stage):
        by_core = self.stages[stage]
        return lax.ppermute(x, "row", [(r, r ^ (1 << by_core[r & 1])) for r in range(self.count)])

    def side(self, stage):
        b0, b1 = self.stages[stage]
        return jnp.where(self.me & 1 == 0, (self.me >> b0) & 1, (self.me >> b1) & 1)

    def halve(self, x, stage):
        h = x.shape[0] // 2
        s = self.side(stage)
        got = self.swap(lax.dynamic_slice_in_dim(x, (1 - s) * h, h), stage)
        return lax.dynamic_slice_in_dim(x, s * h, h) + got

    def double(self, x, stage):
        got = self.swap(x, stage)
        return jnp.where(self.side(stage) == 0, jnp.concatenate([x, got]), jnp.concatenate([got, x]))

    def sum_large(self, x):
        for s in range(len(self.stages)):
            x = self.halve(x, s)
        for s in reversed(range(len(self.stages))):
            x = self.double(x, s)
        return x

    def sum_small(self, x):
        x = self.halve(x, 0)
        for s in range(1, len(self.stages)):
            x = x + self.swap(x, s)
        return self.double(x, 0)


def per_device(shape, panel, trailing):
    p_own, t_t = panel.T, trailing.T
    rows = Rows(shape["row"])
    z, nz = lax.axis_index("col"), shape["col"]
    w, k = p_own.shape
    n = w * nz
    if nz == 4:
        def z_send(x, pairs):
            return lax.ppermute(x, "col", pairs)

        pair = z_send(p_own, [(0, 1), (1, 0), (2, 3), (3, 2)])
        across = z_send(p_own, [(0, 3), (3, 0), (1, 2), (2, 1)])
        inner = z_send(pair, [(1, 2), (2, 1)])
        outer = z_send(across, [(1, 0), (2, 3)])
        far = jnp.where((z == 1) | (z == 2), inner, outer)
        odd = z & 1 == 1
        near = jnp.where(odd, jnp.concatenate([pair, p_own]), jnp.concatenate([p_own, pair]))
        rest = jnp.where(odd, jnp.concatenate([across, far]), jnp.concatenate([far, across]))
        first = z >> 1
        p_full = jnp.where(first == 0, jnp.concatenate([near, rest]), jnp.concatenate([rest, near]))
    else:
        p_full = lax.all_gather(p_own, "col", axis=0, tiled=True)
        near, rest = p_full[: n // 2], p_full[n // 2 :]
        first = jnp.int32(0)
    c_near = rows.sum_large(cross(near, t_t))
    g = rows.sum_small(gram(p_full))
    c_rest = rows.sum_large(cross(rest, t_t))
    lh, ll, qh, ql = factor(g, p_full)
    projections, r_t = update(first.reshape(1), lh, ll, qh, ql, c_near, c_rest, t_t)
    return projections, r_t.T


def solution(mesh):
    return jax.shard_map(
        functools.partial(per_device, dict(mesh.shape)),
        mesh=mesh,
        in_specs=(P("row", "col"), P("row", "col")),
        out_specs=(P("col", None), P("row", "col")),
        check_vma=False,
    )
```

```python
import functools

import jax
import jax.numpy as jnp
from jax import lax
from jax.experimental import pallas as pl
from jax.experimental.pallas import tpu as pltpu
from jax.sharding import PartitionSpec as P

F32, BF16 = jnp.float32, jnp.bfloat16
HIGHEST = lax.Precision.HIGHEST
NT, NN, TN = ((1,), (1,)), ((1,), (0,)), ((0,), (0,))
LANES, NB = 128, 64
VMEM_LIMIT = 12 * 2**20


def dot(a, b, dims, precision=None):
    return lax.dot_general(a, b, (dims, ((), ())), precision=precision, preferred_element_type=F32)


def split(x):
    hi = x.astype(BF16)
    return hi, (x - hi.astype(F32)).astype(BF16)


def params():
    return pltpu.CompilerParams(vmem_limit_bytes=VMEM_LIMIT)


def cost():
    return None


VM = pl.BlockSpec(memory_space=pltpu.VMEM)
HBM = pl.BlockSpec(memory_space=pltpu.HBM)
SMEM = pl.BlockSpec(memory_space=pltpu.SMEM)


def block_rows(m):
    for b in (752, 376):
        if m % b == 0:
            return b
    return m


Z, ODD, FIRST, OTHER, SIDE = 0, 1, 2, 3, 4


def touch_kernel(at_ref, p_ref, t_ref, o_ref, p_out, zero_ref):
    for i in range(at_ref.shape[0]):
        o_ref[i] = at_ref[i]
    p_out[...] = p_ref[...]
    zero_ref[...] = jnp.zeros_like(zero_ref)


def touch(at, p_t, t):
    return pl.pallas_call(
        touch_kernel,
        out_shape=[jax.ShapeDtypeStruct(s, d) for s, d in ((at.shape, jnp.int32), (p_t.shape, F32), (p_t.shape, F32))],
        in_specs=[SMEM, VM, VM],
        out_specs=[SMEM, VM, VM],
        compiler_params=params(),
        cost_estimate=cost(),
        name="touch",
    )(at, p_t, t)


def cross_kernel(at_ref, pa_ref, pb_ref, t_ref, *c_refs, mine):
    n = 2 * pa_ref.shape[0]
    m = c_refs[0].shape[0]
    b = block_rows(m)
    pa, pb = pa_ref[...], pb_ref[...]
    swap = at_ref[ODD] != 0
    p_hi, p_lo = split(jnp.concatenate([jnp.where(swap, pb, pa), jnp.where(swap, pa, pb)], axis=0))
    both = jnp.concatenate([p_hi, p_lo], axis=0)
    for c_ref, own in zip(c_refs, mine):
        half = at_ref[SIDE] if own else 1 - at_ref[SIDE]
        base = pl.multiple_of(half * m, 8)
        for i in range(m // b):
            t_hi, t_lo = split(t_ref[pl.ds(base + i * b, b), :])
            c = dot(t_hi, both, NT)
            c_ref[i * b : (i + 1) * b, :] = c[:, :n] + c[:, n:] + dot(t_lo, p_hi, NT)


def cross(at, mine, pa, pb, t):
    return pl.pallas_call(
        functools.partial(cross_kernel, mine=mine),
        out_shape=[jax.ShapeDtypeStruct((t.shape[0] // 2, 2 * pa.shape[0]), F32)] * len(mine),
        in_specs=[SMEM, VM, VM, VM],
        out_specs=[VM] * len(mine),
        compiler_params=params(),
        cost_estimate=cost(),
        name="cross",
    )(at, pa, pb, t)


def gram_kernel(at_ref, own, pair, far, across, p_full, g_ref):
    w = own.shape[0]
    z = at_ref[Z]
    for flip, block in enumerate((own, pair, far, across)):
        p_full[pl.ds(pl.multiple_of((z ^ flip) * w, 8), w), :] = block[...]
    p = p_full[...]
    g_ref[...] = dot(p, p, NT, HIGHEST)


def gram4(at, *blocks):
    w, k = blocks[0].shape
    return pl.pallas_call(
        gram_kernel,
        out_shape=[jax.ShapeDtypeStruct((4 * w, k), F32), jax.ShapeDtypeStruct((4 * w, 4 * w), F32)],
        in_specs=[SMEM] + [VM] * 4,
        out_specs=[VM] * 2,
        compiler_params=params(),
        cost_estimate=cost(),
        name="gram",
    )(at, *blocks)


def plain_gram_kernel(p_ref, g_ref):
    p = p_ref[...]
    g_ref[...] = dot(p, p, NT, HIGHEST)


def plain_gram(p_t):
    n = p_t.shape[0]
    return pl.pallas_call(
        plain_gram_kernel,
        out_shape=jax.ShapeDtypeStruct((n, n), F32),
        in_specs=[VM],
        out_specs=VM,
        compiler_params=params(),
        cost_estimate=cost(),
        name="gram",
    )(p_t)


def tile(x):
    return jnp.broadcast_to(x, (8, LANES))


def eliminate(rows):
    sub = lax.broadcasted_iota(jnp.int32, (8, LANES), 0)
    n = len(rows)
    scaled = []
    for g in range(n):
        cols = [[tile(rows[i][:, 8 * g + c : 8 * g + c + 1]) for i in range(g, n)] for c in range(8)]
        own = rows[g]
        pivots = jnp.ones((8, LANES), F32)
        factors, lines = [], []
        for c in range(8):
            pivot = tile(cols[c][0][c : c + 1, :])
            inv = 1.0 / pivot
            f = [x * inv for x in cols[c]]
            f[0] = jnp.where(sub > c, f[0], 0.0)
            pivots = jnp.where(sub == c, pivot, pivots)
            for later in range(c + 1, 8):
                e = tile(cols[later][0][c : c + 1, :])
                cols[later] = [x - y * e for x, y in zip(cols[later], f)]
            line = tile(own[c : c + 1, :])
            own = own - f[0] * line
            factors.append(f)
            lines.append(line)
        for i in range(g + 1, n):
            for c in range(8):
                rows[i] = rows[i] - factors[c][i - g] * lines[c]
        scaled.append(own * lax.rsqrt(pivots))
    return scaled


def factor_kernel(s_ref, *rest, first, last):
    left = s_ref.shape[0]
    if first:
        x_ref, *rest = rest
        j0 = lax.broadcasted_iota(jnp.int32, (left, left), 0)
        j1 = lax.broadcasted_iota(jnp.int32, (left, left), 1)
        right = (j0 == j1).astype(F32)
    else:
        r_ref, x_ref, *rest = rest
        right = r_ref[...]
    i0 = lax.broadcasted_iota(jnp.int32, (NB, NB), 0)
    i1 = lax.broadcasted_iota(jnp.int32, (NB, NB), 1)
    eye = (i0 == i1).astype(F32)
    augmented = jnp.concatenate([s_ref[:NB, :NB], eye], axis=1)
    rows = eliminate([augmented[8 * i : 8 * i + 8] for i in range(NB // 8)])
    inv = jnp.concatenate(rows, axis=0)[:, NB:]
    x = dot(inv, right[:NB, :], NN, HIGHEST)
    x_ref[...] = x
    if not last:
        s_out, r_out = rest
        u = dot(inv, s_ref[:NB, NB:], NN, HIGHEST)
        s_out[...] = s_ref[NB:, NB:] - dot(u, u, TN, HIGHEST)
        r_out[...] = right[NB:, :] - dot(u, x, TN, HIGHEST)


def factor_step(s, r=None):
    left = s.shape[0]
    n = left if r is None else r.shape[1]
    last = left == NB
    outs = [jax.ShapeDtypeStruct((NB, n), F32)]
    if not last:
        outs += [jax.ShapeDtypeStruct((left - NB, left - NB), F32), jax.ShapeDtypeStruct((left - NB, n), F32)]
    return pl.pallas_call(
        functools.partial(factor_kernel, first=r is None, last=last),
        out_shape=outs,
        in_specs=[VM] * (1 if r is None else 2),
        out_specs=[VM] * len(outs),
        compiler_params=params(),
        cost_estimate=cost(),
        name="factor",
    )(s, *(() if r is None else (r,)))


def finish_kernel(x0, x1, x2, x3, p_ref, lh_ref, ll_ref, qh_ref, ql_ref):
    linv = jnp.concatenate([x0[...], x1[...], x2[...], x3[...]], axis=0)
    lh_ref[...], ll_ref[...] = split(linv)
    qh_ref[...], ql_ref[...] = split(dot(linv, p_ref[...], NN, HIGHEST))


def finish(xs, p_t):
    n, k = p_t.shape
    return pl.pallas_call(
        finish_kernel,
        out_shape=[jax.ShapeDtypeStruct((n, n), BF16)] * 2 + [jax.ShapeDtypeStruct((n, k), BF16)] * 2,
        in_specs=[VM] * 5,
        out_specs=[VM] * 4,
        compiler_params=params(),
        cost_estimate=cost(),
        name="finish",
    )(*xs, p_t)


def update_kernel(at_ref, lh_ref, ll_ref, qh_ref, ql_ref, *refs, places, into):
    c_refs, t_ref = refs[: len(places)], refs[len(places)]
    p_out, r_out, p_buf, r_buf, sems = refs[len(places) + 1 + into :]
    b = p_buf.shape[1]
    half = t_ref.shape[0] // 2
    lh, ll, qh, ql = lh_ref[...], ll_ref[...], qh_ref[...], ql_ref[...]
    pending = []
    for c_ref, core in zip(c_refs, places):
        start = pl.multiple_of((at_ref[SIDE] ^ core) * half, 8)
        for i in range(c_ref.shape[0] // b):
            s = len(pending) % 2
            there = pl.ds(start + i * b, b)
            c_hi, c_lo = split(c_ref[i * b : (i + 1) * b, :])
            p = dot(c_hi, lh, NT) + dot(c_lo, lh, NT) + dot(c_hi, ll, NT)
            p_hi, p_lo = split(p)
            r = t_ref[there, :] - (dot(p_hi, qh, NN) + dot(p_lo, qh, NN) + dot(p_hi, ql, NN))
            if len(pending) >= 2:
                for c in pending[-2]:
                    c.wait()
            p_buf[s] = p
            r_buf[s] = r
            copies = [
                pltpu.make_async_copy(p_buf.at[s], p_out.at[there], sems.at[0, s]),
                pltpu.make_async_copy(r_buf.at[s], r_out.at[there], sems.at[1, s]),
            ]
            for c in copies:
                c.start()
            pending.append(copies)
    for copies in pending[-2:]:
        for c in copies:
            c.wait()


def update(at, parts, pieces, t, into=()):
    n, k = parts[2].shape
    m = t.shape[0]
    b = block_rows(next(iter(pieces.values())).shape[0])
    return pl.pallas_call(
        functools.partial(update_kernel, places=tuple(pieces), into=len(into)),
        out_shape=[jax.ShapeDtypeStruct((m, n), F32), jax.ShapeDtypeStruct((m, k), F32)],
        in_specs=[SMEM] + [VM] * (5 + len(pieces)) + [HBM] * len(into),
        out_specs=[HBM, HBM],
        scratch_shapes=[pltpu.VMEM((2, b, n), F32), pltpu.VMEM((2, b, k), F32), pltpu.SemaphoreType.DMA((2, 2))],
        input_output_aliases={6 + len(pieces) + i: i for i in range(len(into))},
        compiler_params=params(),
        cost_estimate=cost(),
        name="update",
    )(at, *parts, *pieces.values(), t, *into)


class Rows:
    def __init__(self, count):
        self.count = count
        bits = list(range(1, count.bit_length() - 1))
        self.stages = [(0, 0)] + list(zip(bits, bits[::-1]))

    def swap(self, x, stage):
        by_core = self.stages[stage]
        return lax.ppermute(x, "row", [(r, r ^ (1 << by_core[r & 1])) for r in range(self.count)])

    def place(self, nz):
        me, z = lax.axis_index("row"), lax.axis_index("col")

        def sides(r):
            return [jnp.where(r & 1 == 0, (r >> b0) & 1, (r >> b1) & 1) for b0, b1 in self.stages]

        own = sides(me)
        flags = [z, z & 1, z >> 1] if nz == 4 else [z, 0, 0]
        at = jnp.stack([jnp.asarray(x, jnp.int32) for x in flags + [sides(me ^ 1)[1]] + own])
        return at, [jnp.broadcast_to(s == 1, (1, LANES)) for s in [flags[2]] + own]


class Order:
    def __init__(self):
        self.last = None

    def gate(self, x):
        return x if self.last is None else lax.optimization_barrier((x, self.last))[0]

    def run(self, f, x, *args):
        out = f(self.gate(x), *args)
        self.last = out[0] if isinstance(out, (list, tuple)) else out
        return out


def pick(flag, x, y):
    flag = jnp.broadcast_to(flag[:, :1], x.shape)
    return jnp.where(flag, y, x), jnp.where(flag, x, y)


def per_device(shape, panel, trailing):
    rows = Rows(shape["row"])
    end = len(rows.stages) - 1
    nz = shape["col"]
    at, upper = rows.place(nz)
    p_first = panel.T
    panel, trailing, at, upper = lax.optimization_barrier((panel, trailing, at, upper))
    p_own, t = panel.T, trailing.T
    n = p_own.shape[0] * nz
    second, *upper = upper

    def halved(stage, x, *more):
        h = x.shape[0] // 2
        low, high = x[:h], x[h:]
        for y in more:
            low, high = low + y[:h], high + y[h:]
        return pick(upper[stage], low, high)

    def joined(stage, x, got):
        return jnp.concatenate(pick(upper[stage], x, got))

    o = Order()

    def send(x, stage):
        x = o.gate(x)
        o.last = x
        return rows.swap(x, stage)

    def add(x, y):
        return o.run(lambda x: x + y, x)

    def cut(stage, x, *more):
        return o.run(lambda x: halved(stage, x, *more), x)

    def put(stage, x, got):
        return o.run(lambda x: joined(stage, x, got), x)

    if nz == 4:
        def flipped(x, flip):
            return lax.ppermute(x, "col", [(z, z ^ flip) for z in range(nz)])

        pair, far = flipped(p_first, 1), flipped(p_own, 2)
        at, p_own, zero = touch(at, p_own, t)
        far = far + zero
        across = flipped(far, 1)
        o.last = far
        out_a, a = o.run(lambda x: cross(at, (False, True), x, pair, t), p_own)
        rest = (far, across)
    else:
        p_full = lax.all_gather(p_own, "col", axis=0, tiled=True)
        near, rest = [[p_full[i * (n // 4) : (i + 1) * (n // 4)] for i in h] for h in ((0, 1), (2, 3))]
        out_a, a = cross(at, (False, True), *near, t)
    if nz == 4:
        p_full, g = o.run(lambda x: gram4(at, x, pair, far, across), p_own)
        o.last = g
    else:
        g = o.run(plain_gram, p_full)
    g, out = cut(0, g)
    got_g = send(out, 0)
    got_a = send(out_a, 0)
    g = add(g, got_g)
    got_g = send(g, 1)
    a = add(a, got_a)
    got_a = send(a, 1)
    out_b, b = o.run(lambda x: cross(at, (False, True), x, rest[1], t), rest[0])
    for s in range(2, end + 1):
        g = add(g, got_g)
        got_g = send(g, s)
    got_b = send(out_b, 0)
    for s in range(2, end + 1):
        a = add(a, got_a)
        got_a = send(a, s)
    b = add(b, got_b)
    got_b = send(b, 1)
    g = add(g, got_g)
    g = put(0, g, send(g, 0))
    x0, g, r = o.run(factor_step, g)
    x1, g, r = o.run(factor_step, g, r)
    for s in range(2, end + 1):
        b = add(b, got_b)
        got_b = send(b, s)
    a = add(a, got_a)
    x2, g, r = o.run(factor_step, g, r)
    (x3,) = o.run(factor_step, g, r)
    parts = o.run(lambda x: finish((x0, x1, x2, x3), x), p_full)
    b = add(b, got_b)
    c = o.run(lambda x: jnp.concatenate(pick(second, a, x), axis=1), b)
    c_core = send(c, 0)
    outs = o.run(lambda x: update(at, parts, {0: x}, t), c)
    projections, r_t = o.run(lambda x: update(at, parts, {1: x}, t, outs), c_core)
    return projections, r_t.T


def solution(mesh):
    return jax.shard_map(
        functools.partial(per_device, dict(mesh.shape)),
        mesh=mesh,
        in_specs=(P("row", "col"), P("row", "col")),
        out_specs=(P("col", None), P("row", "col")),
        check_vma=False,
    )
```

```python
import functools

import jax
import jax.numpy as jnp
from jax import lax
from jax.experimental import pallas as pl
from jax.experimental.pallas import tpu as pltpu
from jax.sharding import PartitionSpec as P

F32, BF16 = jnp.float32, jnp.bfloat16
HIGHEST = lax.Precision.HIGHEST
NT, NN, TN = ((1,), (1,)), ((1,), (0,)), ((0,), (0,))
LANES, NB = 128, 64
VMEM_LIMIT = 16 * 2**20


def dot(a, b, dims, precision=None):
    return lax.dot_general(a, b, (dims, ((), ())), precision=precision, preferred_element_type=F32)


def split(x):
    hi = x.astype(BF16)
    return hi, (x - hi.astype(F32)).astype(BF16)


def params():
    return pltpu.CompilerParams(vmem_limit_bytes=VMEM_LIMIT)


def cost():
    return None


VM = pl.BlockSpec(memory_space=pltpu.VMEM)
HBM = pl.BlockSpec(memory_space=pltpu.HBM)
SMEM = pl.BlockSpec(memory_space=pltpu.SMEM)


def block_rows(m):
    for b in (752, 376):
        if m % b == 0:
            return b
    return m


Z, ODD, FIRST, OTHER, SIDE = 0, 1, 2, 3, 4


def touch_kernel(at_ref, p_ref, t_ref, o_ref, p_out, zero_ref):
    for i in range(at_ref.shape[0]):
        o_ref[i] = at_ref[i]
    p_out[...] = p_ref[...]
    zero_ref[...] = jnp.zeros_like(zero_ref)


def touch(at, p_t, t):
    return pl.pallas_call(
        touch_kernel,
        out_shape=[jax.ShapeDtypeStruct(s, d) for s, d in ((at.shape, jnp.int32), (p_t.shape, F32), (p_t.shape, F32))],
        in_specs=[SMEM, VM, VM],
        out_specs=[SMEM, VM, VM],
        compiler_params=params(),
        cost_estimate=cost(),
        name="touch",
    )(at, p_t, t)


def cross_kernel(at_ref, pa_ref, pb_ref, t_ref, *c_refs, mine):
    n = 2 * pa_ref.shape[0]
    m = c_refs[0].shape[0]
    b = block_rows(m)
    pa, pb = pa_ref[...], pb_ref[...]
    swap = at_ref[ODD] != 0
    p_hi, p_lo = split(jnp.concatenate([jnp.where(swap, pb, pa), jnp.where(swap, pa, pb)], axis=0))
    both = jnp.concatenate([p_hi, p_lo], axis=0)
    for c_ref, own in zip(c_refs, mine):
        half = at_ref[SIDE] if own else 1 - at_ref[SIDE]
        base = pl.multiple_of(half * m, 8)
        for i in range(m // b):
            t_hi, t_lo = split(t_ref[pl.ds(base + i * b, b), :])
            c = dot(t_hi, both, NT)
            c_ref[i * b : (i + 1) * b, :] = c[:, :n] + c[:, n:] + dot(t_lo, p_hi, NT)


def cross(at, mine, pa, pb, t):
    return pl.pallas_call(
        functools.partial(cross_kernel, mine=mine),
        out_shape=[jax.ShapeDtypeStruct((t.shape[0] // 2, 2 * pa.shape[0]), F32)] * len(mine),
        in_specs=[SMEM, VM, VM, VM],
        out_specs=[VM] * len(mine),
        compiler_params=params(),
        cost_estimate=cost(),
        name="cross",
    )(at, pa, pb, t)


def gram_kernel(at_ref, own, pair, far, across, p_full, g_ref):
    w = own.shape[0]
    z = at_ref[Z]
    for flip, block in enumerate((own, pair, far, across)):
        p_full[pl.ds(pl.multiple_of((z ^ flip) * w, 8), w), :] = block[...]
    p = p_full[...]
    g_ref[...] = dot(p, p, NT, HIGHEST)


def gram4(at, *blocks):
    w, k = blocks[0].shape
    return pl.pallas_call(
        gram_kernel,
        out_shape=[jax.ShapeDtypeStruct((4 * w, k), F32), jax.ShapeDtypeStruct((4 * w, 4 * w), F32)],
        in_specs=[SMEM] + [VM] * 4,
        out_specs=[VM] * 2,
        compiler_params=params(),
        cost_estimate=cost(),
        name="gram",
    )(at, *blocks)


def plain_gram_kernel(p_ref, g_ref):
    p = p_ref[...]
    g_ref[...] = dot(p, p, NT, HIGHEST)


def plain_gram(p_t):
    n = p_t.shape[0]
    return pl.pallas_call(
        plain_gram_kernel,
        out_shape=jax.ShapeDtypeStruct((n, n), F32),
        in_specs=[VM],
        out_specs=VM,
        compiler_params=params(),
        cost_estimate=cost(),
        name="gram",
    )(p_t)


def tile(x):
    return jnp.broadcast_to(x, (8, LANES))


def eliminate(rows):
    sub = lax.broadcasted_iota(jnp.int32, (8, LANES), 0)
    n = len(rows)
    scaled = []
    for g in range(n):
        cols = [[tile(rows[i][:, 8 * g + c : 8 * g + c + 1]) for i in range(g, n)] for c in range(8)]
        own = rows[g]
        pivots = jnp.ones((8, LANES), F32)
        factors, lines = [], []
        for c in range(8):
            pivot = tile(cols[c][0][c : c + 1, :])
            inv = 1.0 / pivot
            f = [x * inv for x in cols[c]]
            f[0] = jnp.where(sub > c, f[0], 0.0)
            pivots = jnp.where(sub == c, pivot, pivots)
            for later in range(c + 1, 8):
                e = tile(cols[later][0][c : c + 1, :])
                cols[later] = [x - y * e for x, y in zip(cols[later], f)]
            line = tile(own[c : c + 1, :])
            own = own - f[0] * line
            factors.append(f)
            lines.append(line)
        for i in range(g + 1, n):
            for c in range(8):
                rows[i] = rows[i] - factors[c][i - g] * lines[c]
        scaled.append(own * lax.rsqrt(pivots))
    return scaled


def factor_kernel(s_ref, *rest, first, last):
    left = s_ref.shape[0]
    if first:
        x_ref, *rest = rest
        j0 = lax.broadcasted_iota(jnp.int32, (left, left), 0)
        j1 = lax.broadcasted_iota(jnp.int32, (left, left), 1)
        right = (j0 == j1).astype(F32)
    else:
        r_ref, x_ref, *rest = rest
        right = r_ref[...]
    i0 = lax.broadcasted_iota(jnp.int32, (NB, NB), 0)
    i1 = lax.broadcasted_iota(jnp.int32, (NB, NB), 1)
    eye = (i0 == i1).astype(F32)
    augmented = jnp.concatenate([s_ref[:NB, :NB], eye], axis=1)
    rows = eliminate([augmented[8 * i : 8 * i + 8] for i in range(NB // 8)])
    inv = jnp.concatenate(rows, axis=0)[:, NB:]
    x = dot(inv, right[:NB, :], NN, HIGHEST)
    x_ref[...] = x
    if not last:
        s_out, r_out = rest
        u = dot(inv, s_ref[:NB, NB:], NN, HIGHEST)
        s_out[...] = s_ref[NB:, NB:] - dot(u, u, TN, HIGHEST)
        r_out[...] = right[NB:, :] - dot(u, x, TN, HIGHEST)


def factor_step(s, r=None):
    left = s.shape[0]
    n = left if r is None else r.shape[1]
    last = left == NB
    outs = [jax.ShapeDtypeStruct((NB, n), F32)]
    if not last:
        outs += [jax.ShapeDtypeStruct((left - NB, left - NB), F32), jax.ShapeDtypeStruct((left - NB, n), F32)]
    return pl.pallas_call(
        functools.partial(factor_kernel, first=r is None, last=last),
        out_shape=outs,
        in_specs=[VM] * (1 if r is None else 2),
        out_specs=[VM] * len(outs),
        compiler_params=params(),
        cost_estimate=cost(),
        name="factor",
    )(s, *(() if r is None else (r,)))


def finish_kernel(x0, x1, x2, x3, p_ref, lh_ref, ll_ref, qh_ref, ql_ref):
    linv = jnp.concatenate([x0[...], x1[...], x2[...], x3[...]], axis=0)
    lh_ref[...], ll_ref[...] = split(linv)
    qh_ref[...], ql_ref[...] = split(dot(linv, p_ref[...], NN, HIGHEST))


def finish(xs, p_t):
    n, k = p_t.shape
    return pl.pallas_call(
        finish_kernel,
        out_shape=[jax.ShapeDtypeStruct((n, n), BF16)] * 2 + [jax.ShapeDtypeStruct((n, k), BF16)] * 2,
        in_specs=[VM] * 5,
        out_specs=[VM] * 4,
        compiler_params=params(),
        cost_estimate=cost(),
        name="finish",
    )(*xs, p_t)


def quarter_start(at_ref, place, rows):
    core, chip = place
    side = at_ref[OTHER if core else SIDE + 1]
    return pl.multiple_of((at_ref[SIDE] ^ core) * (rows // 2) + (side ^ chip) * (rows // 4), 8)


def update_kernel(at_ref, lh_ref, ll_ref, qh_ref, ql_ref, *refs, places, carried, into, last):
    c_refs, refs = refs[: len(places)], refs[len(places) :]
    t_ref, refs = refs[0], refs[1:]
    carry, refs = (refs[:2], refs[2:]) if carried else ((), refs)
    outs = refs[into:]
    rows = t_ref.shape[0]
    copies = []
    if last:
        p_out, r_out, *outs = outs
        sems = refs[-1]
    if carried:
        m = carry[0].shape[0] // len(carried)
        for j, place in enumerate(carried):
            here, there = pl.ds(j * m, m), pl.ds(quarter_start(at_ref, place, rows), m)
            copies += [
                pltpu.make_async_copy(carry[0].at[here], p_out.at[there], sems.at[0, j]),
                pltpu.make_async_copy(carry[1].at[here], r_out.at[there], sems.at[1, j]),
            ]
        for c in copies:
            c.start()
    p_here, r_here = outs[:2]
    lh, ll, qh, ql = lh_ref[...], ll_ref[...], qh_ref[...], ql_ref[...]
    m = c_refs[0].shape[0]
    b = m // 2 if last and m % 16 == 0 else m
    for j, (c_ref, place) in enumerate(zip(c_refs, places)):
        start = quarter_start(at_ref, place, rows)
        for i in range(m // b):
            here, there = pl.ds(j * m + i * b, b), pl.ds(start + i * b, b)
            c_hi, c_lo = split(c_ref[i * b : (i + 1) * b, :])
            p = dot(c_hi, lh, NT) + dot(c_lo, lh, NT) + dot(c_hi, ll, NT)
            p_here[here, :] = p
            p_hi, p_lo = split(p)
            r_here[here, :] = t_ref[there, :] - (dot(p_hi, qh, NN) + dot(p_lo, qh, NN) + dot(p_hi, ql, NN))
            if last:
                s = len(carried) + j * (m // b) + i
                copies += [
                    pltpu.make_async_copy(p_here.at[here], p_out.at[there], sems.at[0, s]),
                    pltpu.make_async_copy(r_here.at[here], r_out.at[there], sems.at[1, s]),
                ]
                for c in copies[-2:]:
                    c.start()
    for c in copies:
        c.wait()


def update(at, parts, pieces, t, carried=(), carry=(), into=(), last=True):
    n, k = parts[2].shape
    m = t.shape[0]
    h = sum(x.shape[0] for x in pieces.values())
    own = [((h, n), F32), ((h, k), F32)]
    if last:
        out = [jax.ShapeDtypeStruct((m, n), F32), jax.ShapeDtypeStruct((m, k), F32)]
        scratch = [pltpu.VMEM(*x) for x in own] + [pltpu.SemaphoreType.DMA((2, len(carried) + 2 * len(pieces)))]
    else:
        out, scratch = [jax.ShapeDtypeStruct(*x) for x in own], []
    inputs = [at, *parts, *pieces.values(), t, *carry]
    return pl.pallas_call(
        functools.partial(update_kernel, places=tuple(pieces), carried=carried, into=len(into), last=last),
        out_shape=out,
        in_specs=[SMEM] + [VM] * (len(inputs) - 1) + [HBM] * len(into),
        out_specs=[HBM if last else VM] * 2,
        scratch_shapes=scratch,
        input_output_aliases={len(inputs) + i: i for i in range(len(into))},
        compiler_params=params(),
        cost_estimate=cost(),
        name="update",
    )(*inputs, *into)


class Rows:
    def __init__(self, count):
        self.count = count
        bits = list(range(1, count.bit_length() - 1))
        self.stages = [(0, 0)] + list(zip(bits, bits[::-1]))

    def swap(self, x, stage):
        by_core = self.stages[stage]
        return lax.ppermute(x, "row", [(r, r ^ (1 << by_core[r & 1])) for r in range(self.count)])

    def place(self, nz):
        me, z = lax.axis_index("row"), lax.axis_index("col")

        def sides(r):
            return [jnp.where(r & 1 == 0, (r >> b0) & 1, (r >> b1) & 1) for b0, b1 in self.stages]

        own = sides(me)
        flags = [z, z & 1, z >> 1] if nz == 4 else [z, 0, 0]
        at = jnp.stack([jnp.asarray(x, jnp.int32) for x in flags + [sides(me ^ 1)[1]] + own])
        return at, [jnp.broadcast_to(s == 1, (1, LANES)) for s in [flags[2]] + own]


class Order:
    def __init__(self):
        self.last = None

    def gate(self, x):
        return x if self.last is None else lax.optimization_barrier((x, self.last))[0]

    def run(self, f, x, *args):
        out = f(self.gate(x), *args)
        self.last = out[0] if isinstance(out, (list, tuple)) else out
        return out


def pick(flag, x, y):
    flag = jnp.broadcast_to(flag[:, :1], x.shape)
    return jnp.where(flag, y, x), jnp.where(flag, x, y)


def per_device(shape, panel, trailing):
    rows = Rows(shape["row"])
    end = len(rows.stages) - 1
    nz = shape["col"]
    at, upper = rows.place(nz)
    p_first = panel.T
    panel, trailing, at, upper = lax.optimization_barrier((panel, trailing, at, upper))
    p_own, t = panel.T, trailing.T
    n = p_own.shape[0] * nz
    second, *upper = upper

    def halved(stage, x, *more):
        h = x.shape[0] // 2
        low, high = x[:h], x[h:]
        for y in more:
            low, high = low + y[:h], high + y[h:]
        return pick(upper[stage], low, high)

    def joined(stage, x, got):
        return jnp.concatenate(pick(upper[stage], x, got))

    o = Order()

    def send(x, stage):
        x = o.gate(x)
        o.last = x
        return rows.swap(x, stage)

    def add(x, y):
        return o.run(lambda x: x + y, x)

    def cut(stage, x, *more):
        return o.run(lambda x: halved(stage, x, *more), x)

    def put(stage, x, got):
        return o.run(lambda x: joined(stage, x, got), x)

    def columns(x, y):
        return o.run(lambda y: jnp.concatenate(pick(second, x, y), axis=1), y)

    if nz == 4:
        def flipped(x, flip):
            return lax.ppermute(x, "col", [(z, z ^ flip) for z in range(nz)])

        pair, far = flipped(p_first, 1), flipped(p_own, 2)
        at, p_own, zero = touch(at, p_own, t)
        far = far + zero
        across = flipped(far, 1)
        o.last = far
        out_a, a = o.run(lambda x: cross(at, (False, True), x, pair, t), p_own)
        rest = (far, across)
    else:
        p_full = lax.all_gather(p_own, "col", axis=0, tiled=True)
        near, rest = [[p_full[i * (n // 4) : (i + 1) * (n // 4)] for i in h] for h in ((0, 1), (2, 3))]
        out_a, a = cross(at, (False, True), *near, t)
    if nz == 4:
        p_full, g = o.run(lambda x: gram4(at, x, pair, far, across), p_own)
        o.last = g
    else:
        g = o.run(plain_gram, p_full)
    g, out = cut(0, g)
    got_g = send(out, 0)
    got_a = send(out_a, 0)
    g = add(g, got_g)
    got_g = send(g, end)
    a, out_a = cut(1, a, got_a)
    got_a = send(out_a, 1)
    out_b, b = o.run(lambda x: cross(at, (False, True), x, rest[1], t), rest[0])
    for s in range(end - 1, 0, -1):
        g = add(g, got_g)
        got_g = send(g, s)
    for s in range(2, end):
        a, out_a = cut(s, a, got_a)
        got_a = send(out_a, s)
    a = add(a, got_a)
    got_a = send(a, end)
    b, out_b = cut(1, b, send(out_b, 0))
    got_b = send(out_b, 1)
    a = add(a, got_a)
    for s in range(end - 1, 1, -1):
        a = put(s, a, send(a, s))
    for s in range(2, end):
        b, out_b = cut(s, b, got_b)
        got_b = send(out_b, s)
    b = add(b, got_b)
    g = add(g, got_g)
    got_g = send(g, 0)
    got_b = send(b, end)
    a_chip = send(a, 1)
    g = put(0, g, got_g)
    x0, g, r = o.run(factor_step, g)
    x1, g, r = o.run(factor_step, g, r)
    x2, g, r = o.run(factor_step, g, r)
    (x3,) = o.run(factor_step, g, r)
    o.last = (x3, a_chip)
    b = add(b, got_b)
    for s in range(end - 1, 1, -1):
        b = put(s, b, send(b, s))
    b_chip = send(b, 1)
    c = columns(a, b)
    c_core = send(c, 0)
    parts = o.run(lambda x: finish((x0, x1, x2, x3), x), p_full)
    outs = o.run(lambda x: update(at, parts, {(0, 0): c, (1, 0): x}, t), c_core)
    c_chip = columns(a_chip, b_chip)
    c_both = send(c_chip, 0)
    carry = o.run(lambda x: update(at, parts, {(0, 1): x}, t, last=False), c_chip)
    projections, r_t = update(at, parts, {(1, 1): c_both}, t, ((0, 1),), carry, outs)
    return projections, r_t.T


def solution(mesh):
    return jax.shard_map(
        functools.partial(per_device, dict(mesh.shape)),
        mesh=mesh,
        in_specs=(P("row", "col"), P("row", "col")),
        out_specs=(P("col", None), P("row", "col")),
        check_vma=False,
    )
```

```python
import functools

import jax
import jax.numpy as jnp
from jax import lax
from jax.experimental import pallas as pl
from jax.experimental.pallas import tpu as pltpu
from jax.sharding import PartitionSpec as P

F32, BF16 = jnp.float32, jnp.bfloat16
HIGHEST = lax.Precision.HIGHEST
NT, NN, TN = ((1,), (1,)), ((1,), (0,)), ((0,), (0,))
LANES, NB = 128, 64
VMEM_LIMIT = 16 * 2**20


def dot(a, b, dims, precision=None):
    return lax.dot_general(a, b, (dims, ((), ())), precision=precision, preferred_element_type=F32)


def split(x):
    hi = x.astype(BF16)
    return hi, (x - hi.astype(F32)).astype(BF16)


def params():
    return pltpu.CompilerParams(vmem_limit_bytes=VMEM_LIMIT)


def cost():
    return None


VM = pl.BlockSpec(memory_space=pltpu.VMEM)
HBM = pl.BlockSpec(memory_space=pltpu.HBM)
SMEM = pl.BlockSpec(memory_space=pltpu.SMEM)


def block_rows(m):
    for b in (752, 376):
        if m % b == 0:
            return b
    return m


Z, ODD, FIRST, OTHER, SIDE = 0, 1, 2, 3, 4


def touch_kernel(at_ref, p_ref, t_ref, o_ref, p_out, zero_ref):
    for i in range(at_ref.shape[0]):
        o_ref[i] = at_ref[i]
    p_out[...] = p_ref[...]
    zero_ref[...] = jnp.zeros_like(zero_ref)


def touch(at, p_t, t):
    return pl.pallas_call(
        touch_kernel,
        out_shape=[jax.ShapeDtypeStruct(s, d) for s, d in ((at.shape, jnp.int32), (p_t.shape, F32), (p_t.shape, F32))],
        in_specs=[SMEM, VM, VM],
        out_specs=[SMEM, VM, VM],
        compiler_params=params(),
        cost_estimate=cost(),
        name="touch",
    )(at, p_t, t)


def cross_kernel(at_ref, pa_ref, pb_ref, t_ref, *c_refs, halves):
    n = 2 * pa_ref.shape[0]
    m = t_ref.shape[0] // 2
    b = block_rows(m)
    pa, pb = pa_ref[...], pb_ref[...]
    swap = at_ref[ODD] != 0
    p_hi, p_lo = split(jnp.concatenate([jnp.where(swap, pb, pa), jnp.where(swap, pa, pb)], axis=0))
    both = jnp.concatenate([p_hi, p_lo], axis=0)
    refs = list(c_refs)
    for own, pieces in halves:
        half = at_ref[SIDE] if own else 1 - at_ref[SIDE]
        base = pl.multiple_of(half * m, 8)
        outs, refs = refs[:pieces], refs[pieces:]
        piece = m // pieces
        for i in range(0, m, b):
            t_hi, t_lo = split(t_ref[pl.ds(base + i, b), :])
            c = dot(t_hi, both, NT)
            c = c[:, :n] + c[:, n:] + dot(t_lo, p_hi, NT)
            if pieces == 1:
                outs[0][i : i + b, :] = c
            else:
                for j in range(0, b, piece):
                    outs[(i + j) // piece][...] = c[j : j + piece]


def cross(at, halves, pa, pb, t):
    m, n = t.shape[0] // 2, 2 * pa.shape[0]
    shapes = [(m // pieces, n) for _, pieces in halves for _ in range(pieces)]
    return pl.pallas_call(
        functools.partial(cross_kernel, halves=halves),
        out_shape=[jax.ShapeDtypeStruct(s, F32) for s in shapes],
        in_specs=[SMEM, VM, VM, VM],
        out_specs=[VM] * len(shapes),
        compiler_params=params(),
        cost_estimate=cost(),
        name="cross",
    )(at, pa, pb, t)


def halve_kernel(at_ref, keep_ref, *refs):
    *got_refs, keep_out, send_out = refs
    m = got_refs[0].shape[0]
    upper = at_ref[SIDE + 1] != 0
    h = len(got_refs) // 2
    for j in range(h):
        low = keep_ref[j * m : (j + 1) * m, :] + got_refs[j][...]
        high = keep_ref[(j + h) * m : (j + h + 1) * m, :] + got_refs[j + h][...]
        keep_out[j * m : (j + 1) * m, :] = jnp.where(upper, high, low)
        send_out[j * m : (j + 1) * m, :] = jnp.where(upper, low, high)


def halve(at, keep, got):
    m, n = keep.shape
    return pl.pallas_call(
        halve_kernel,
        out_shape=[jax.ShapeDtypeStruct((m // 2, n), F32)] * 2,
        in_specs=[SMEM] + [VM] * (1 + len(got)),
        out_specs=[VM] * 2,
        compiler_params=params(),
        cost_estimate=cost(),
        name="halve",
    )(at, keep, *got)


def gram_kernel(at_ref, own, pair, far, across, p_full, g_ref):
    w = own.shape[0]
    z = at_ref[Z]
    for flip, block in enumerate((own, pair, far, across)):
        p_full[pl.ds(pl.multiple_of((z ^ flip) * w, 8), w), :] = block[...]
    p = p_full[...]
    g_ref[...] = dot(p, p, NT, HIGHEST)


def gram4(at, *blocks):
    w, k = blocks[0].shape
    return pl.pallas_call(
        gram_kernel,
        out_shape=[jax.ShapeDtypeStruct((4 * w, k), F32), jax.ShapeDtypeStruct((4 * w, 4 * w), F32)],
        in_specs=[SMEM] + [VM] * 4,
        out_specs=[VM] * 2,
        compiler_params=params(),
        cost_estimate=cost(),
        name="gram",
    )(at, *blocks)


def plain_gram_kernel(p_ref, g_ref):
    p = p_ref[...]
    g_ref[...] = dot(p, p, NT, HIGHEST)


def plain_gram(p_t):
    n = p_t.shape[0]
    return pl.pallas_call(
        plain_gram_kernel,
        out_shape=jax.ShapeDtypeStruct((n, n), F32),
        in_specs=[VM],
        out_specs=VM,
        compiler_params=params(),
        cost_estimate=cost(),
        name="gram",
    )(p_t)


def tile(x):
    return jnp.broadcast_to(x, (8, LANES))


def eliminate(rows):
    sub = lax.broadcasted_iota(jnp.int32, (8, LANES), 0)
    n = len(rows)
    scaled = []
    for g in range(n):
        cols = [[tile(rows[i][:, 8 * g + c : 8 * g + c + 1]) for i in range(g, n)] for c in range(8)]
        own = rows[g]
        pivots = jnp.ones((8, LANES), F32)
        factors, lines = [], []
        for c in range(8):
            pivot = tile(cols[c][0][c : c + 1, :])
            inv = 1.0 / pivot
            f = [x * inv for x in cols[c]]
            f[0] = jnp.where(sub > c, f[0], 0.0)
            pivots = jnp.where(sub == c, pivot, pivots)
            for later in range(c + 1, 8):
                e = tile(cols[later][0][c : c + 1, :])
                cols[later] = [x - y * e for x, y in zip(cols[later], f)]
            line = tile(own[c : c + 1, :])
            own = own - f[0] * line
            factors.append(f)
            lines.append(line)
        for i in range(g + 1, n):
            for c in range(8):
                rows[i] = rows[i] - factors[c][i - g] * lines[c]
        scaled.append(own * lax.rsqrt(pivots))
    return scaled


def factor_kernel(s_ref, *rest, first, last):
    left = s_ref.shape[0]
    if first:
        x_ref, *rest = rest
        j0 = lax.broadcasted_iota(jnp.int32, (left, left), 0)
        j1 = lax.broadcasted_iota(jnp.int32, (left, left), 1)
        right = (j0 == j1).astype(F32)
    else:
        r_ref, x_ref, *rest = rest
        right = r_ref[...]
    i0 = lax.broadcasted_iota(jnp.int32, (NB, NB), 0)
    i1 = lax.broadcasted_iota(jnp.int32, (NB, NB), 1)
    eye = (i0 == i1).astype(F32)
    augmented = jnp.concatenate([s_ref[:NB, :NB], eye], axis=1)
    rows = eliminate([augmented[8 * i : 8 * i + 8] for i in range(NB // 8)])
    inv = jnp.concatenate(rows, axis=0)[:, NB:]
    x = dot(inv, right[:NB, :], NN, HIGHEST)
    x_ref[...] = x
    if not last:
        s_out, r_out = rest
        u = dot(inv, s_ref[:NB, NB:], NN, HIGHEST)
        s_out[...] = s_ref[NB:, NB:] - dot(u, u, TN, HIGHEST)
        r_out[...] = right[NB:, :] - dot(u, x, TN, HIGHEST)


def factor_step(s, r=None):
    left = s.shape[0]
    n = left if r is None else r.shape[1]
    last = left == NB
    outs = [jax.ShapeDtypeStruct((NB, n), F32)]
    if not last:
        outs += [jax.ShapeDtypeStruct((left - NB, left - NB), F32), jax.ShapeDtypeStruct((left - NB, n), F32)]
    return pl.pallas_call(
        functools.partial(factor_kernel, first=r is None, last=last),
        out_shape=outs,
        in_specs=[VM] * (1 if r is None else 2),
        out_specs=[VM] * len(outs),
        compiler_params=params(),
        cost_estimate=cost(),
        name="factor",
    )(s, *(() if r is None else (r,)))


def finish_kernel(x0, x1, x2, x3, p_ref, lh_ref, ll_ref, qh_ref, ql_ref):
    linv = jnp.concatenate([x0[...], x1[...], x2[...], x3[...]], axis=0)
    lh_ref[...], ll_ref[...] = split(linv)
    qh_ref[...], ql_ref[...] = split(dot(linv, p_ref[...], NN, HIGHEST))


def finish(xs, p_t):
    n, k = p_t.shape
    return pl.pallas_call(
        finish_kernel,
        out_shape=[jax.ShapeDtypeStruct((n, n), BF16)] * 2 + [jax.ShapeDtypeStruct((n, k), BF16)] * 2,
        in_specs=[VM] * 5,
        out_specs=[VM] * 4,
        compiler_params=params(),
        cost_estimate=cost(),
        name="finish",
    )(*xs, p_t)


def quarter_start(at_ref, place, rows):
    core, chip = place
    side = at_ref[OTHER if core else SIDE + 1]
    return pl.multiple_of((at_ref[SIDE] ^ core) * (rows // 2) + (side ^ chip) * (rows // 4), 8)


def update_kernel(at_ref, lh_ref, ll_ref, qh_ref, ql_ref, *refs, places, carried, into, last):
    c_refs, refs = refs[: len(places)], refs[len(places) :]
    t_ref, refs = refs[0], refs[1:]
    carry, refs = (refs[:2], refs[2:]) if carried else ((), refs)
    outs = refs[into:]
    rows = t_ref.shape[0]
    copies = []
    if last:
        p_out, r_out, *outs = outs
        sems = refs[-1]
    if carried:
        m = carry[0].shape[0] // len(carried)
        for j, place in enumerate(carried):
            here, there = pl.ds(j * m, m), pl.ds(quarter_start(at_ref, place, rows), m)
            copies += [
                pltpu.make_async_copy(carry[0].at[here], p_out.at[there], sems.at[0, j]),
                pltpu.make_async_copy(carry[1].at[here], r_out.at[there], sems.at[1, j]),
            ]
        for c in copies:
            c.start()
    p_here, r_here = outs[:2]
    lh, ll, qh, ql = lh_ref[...], ll_ref[...], qh_ref[...], ql_ref[...]
    m = c_refs[0].shape[0]
    b = m // 2 if last and m % 16 == 0 else m
    for j, (c_ref, place) in enumerate(zip(c_refs, places)):
        start = quarter_start(at_ref, place, rows)
        for i in range(m // b):
            here, there = pl.ds(j * m + i * b, b), pl.ds(start + i * b, b)
            c_hi, c_lo = split(c_ref[i * b : (i + 1) * b, :])
            p = dot(c_hi, lh, NT) + dot(c_lo, lh, NT) + dot(c_hi, ll, NT)
            p_here[here, :] = p
            p_hi, p_lo = split(p)
            r_here[here, :] = t_ref[there, :] - (dot(p_hi, qh, NN) + dot(p_lo, qh, NN) + dot(p_hi, ql, NN))
            if last:
                s = len(carried) + j * (m // b) + i
                copies += [
                    pltpu.make_async_copy(p_here.at[here], p_out.at[there], sems.at[0, s]),
                    pltpu.make_async_copy(r_here.at[here], r_out.at[there], sems.at[1, s]),
                ]
                for c in copies[-2:]:
                    c.start()
    for c in copies:
        c.wait()


def update(at, parts, pieces, t, carried=(), carry=(), into=(), last=True):
    n, k = parts[2].shape
    m = t.shape[0]
    h = sum(x.shape[0] for x in pieces.values())
    own = [((h, n), F32), ((h, k), F32)]
    if last:
        out = [jax.ShapeDtypeStruct((m, n), F32), jax.ShapeDtypeStruct((m, k), F32)]
        scratch = [pltpu.VMEM(*x) for x in own] + [pltpu.SemaphoreType.DMA((2, len(carried) + 2 * len(pieces)))]
    else:
        out, scratch = [jax.ShapeDtypeStruct(*x) for x in own], []
    inputs = [at, *parts, *pieces.values(), t, *carry]
    return pl.pallas_call(
        functools.partial(update_kernel, places=tuple(pieces), carried=carried, into=len(into), last=last),
        out_shape=out,
        in_specs=[SMEM] + [VM] * (len(inputs) - 1) + [HBM] * len(into),
        out_specs=[HBM if last else VM] * 2,
        scratch_shapes=scratch,
        input_output_aliases={len(inputs) + i: i for i in range(len(into))},
        compiler_params=params(),
        cost_estimate=cost(),
        name="update",
    )(*inputs, *into)


class Rows:
    def __init__(self, count):
        self.count = count
        bits = list(range(1, count.bit_length() - 1))
        self.stages = [(0, 0)] + list(zip(bits, bits[::-1]))

    def swap(self, x, stage):
        by_core = self.stages[stage]
        return lax.ppermute(x, "row", [(r, r ^ (1 << by_core[r & 1])) for r in range(self.count)])

    def place(self, nz):
        me, z = lax.axis_index("row"), lax.axis_index("col")

        def sides(r):
            return [jnp.where(r & 1 == 0, (r >> b0) & 1, (r >> b1) & 1) for b0, b1 in self.stages]

        own = sides(me)
        flags = [z, z & 1, z >> 1] if nz == 4 else [z, 0, 0]
        at = jnp.stack([jnp.asarray(x, jnp.int32) for x in flags + [sides(me ^ 1)[1]] + own])
        return at, [jnp.broadcast_to(s == 1, (1, LANES)) for s in [flags[2]] + own]


class Order:
    def __init__(self):
        self.last = None

    def gate(self, x):
        return x if self.last is None else lax.optimization_barrier((x, self.last))[0]

    def run(self, f, x, *args):
        out = f(self.gate(x), *args)
        self.last = out[0] if isinstance(out, (list, tuple)) else out
        return out


def pick(flag, x, y):
    flag = jnp.broadcast_to(flag[:, :1], x.shape)
    return jnp.where(flag, y, x), jnp.where(flag, x, y)


def per_device(shape, panel, trailing):
    rows = Rows(shape["row"])
    end = len(rows.stages) - 1
    nz = shape["col"]
    at, upper = rows.place(nz)
    p_first = panel.T
    panel, trailing, at, upper = lax.optimization_barrier((panel, trailing, at, upper))
    p_own, t = panel.T, trailing.T
    n = p_own.shape[0] * nz
    second, *upper = upper

    def halved(stage, x, *more):
        h = x.shape[0] // 2
        low, high = x[:h], x[h:]
        for y in more:
            low, high = low + y[:h], high + y[h:]
        return pick(upper[stage], low, high)

    def joined(stage, x, got):
        return jnp.concatenate(pick(upper[stage], x, got))

    o = Order()

    def send(x, stage):
        x = o.gate(x)
        o.last = x
        return rows.swap(x, stage)

    def add(x, y):
        return o.run(lambda x: x + y, x)

    def cut(stage, x, *more):
        return o.run(lambda x: halved(stage, x, *more), x)

    def put(stage, x, got):
        return o.run(lambda x: joined(stage, x, got), x)

    def columns(x, y):
        return o.run(lambda y: jnp.concatenate(pick(second, x, y), axis=1), y)

    if nz == 4:
        def flipped(x, flip):
            return lax.ppermute(x, "col", [(z, z ^ flip) for z in range(nz)])

        pair, far = flipped(p_first, 1), flipped(p_own, 2)
        at, p_own, zero = touch(at, p_own, t)
        far = far + zero
        across = flipped(far, 1)
        o.last = far
        *out_a, a = o.run(lambda x: cross(at, ((False, 4), (True, 1)), x, pair, t), p_own)
        rest = (far, across)
    else:
        p_full = lax.all_gather(p_own, "col", axis=0, tiled=True)
        near, rest = [[p_full[i * (n // 4) : (i + 1) * (n // 4)] for i in h] for h in ((0, 1), (2, 3))]
        out_a, a = cross(at, ((False, 1), (True, 1)), *near, t)
    if nz == 4:
        got_a = [rows.swap(x, 0) for x in out_a]
        o.last = (out_a[0], across)
        a, out_a = o.run(lambda x: halve(at, x, got_a), a)
        o.last = out_a
    else:
        a, out_a = cut(1, a, send(out_a, 0))
    got_a = send(out_a, 1)
    if nz == 4:
        p_full, g = o.run(lambda x: gram4(at, x, pair, far, across), p_own)
        o.last = g
    else:
        g = o.run(plain_gram, p_full)
    g, out = cut(0, g)
    got_g = send(out, 0)
    (out_b,) = o.run(lambda x: cross(at, ((False, 1),), x, rest[1], t), rest[0])
    g = add(g, got_g)
    got_g = send(g, 1)
    for s in range(2, end):
        a, out_a = cut(s, a, got_a)
        got_a = send(out_a, s)
    a = add(a, got_a)
    got_a = send(a, end)
    got_b = send(out_b, 0)
    (b,) = o.run(lambda x: cross(at, ((True, 1),), x, rest[1], t), rest[0])
    for s in range(2, end + 1):
        g = add(g, got_g)
        got_g = send(g, s)
    b, out_b = cut(1, b, got_b)
    got_b = send(out_b, 1)
    a = add(a, got_a)
    for s in range(end - 1, 1, -1):
        a = put(s, a, send(a, s))
    for s in range(2, end):
        b, out_b = cut(s, b, got_b)
        got_b = send(out_b, s)
    b = add(b, got_b)
    g = add(g, got_g)
    got_g = send(g, 0)
    got_b = send(b, end)
    a_chip = send(a, 1)
    g = put(0, g, got_g)
    x0, g, r = o.run(factor_step, g)
    x1, g, r = o.run(factor_step, g, r)
    x2, g, r = o.run(factor_step, g, r)
    (x3,) = o.run(factor_step, g, r)
    o.last = (x3, a_chip)
    b = add(b, got_b)
    for s in range(end - 1, 1, -1):
        b = put(s, b, send(b, s))
    b_chip = send(b, 1)
    c = columns(a, b)
    c_core = send(c, 0)
    parts = o.run(lambda x: finish((x0, x1, x2, x3), x), p_full)
    outs = o.run(lambda x: update(at, parts, {(0, 0): c, (1, 0): x}, t), c_core)
    c_chip = columns(a_chip, b_chip)
    c_both = send(c_chip, 0)
    carry = o.run(lambda x: update(at, parts, {(0, 1): x}, t, last=False), c_chip)
    projections, r_t = update(at, parts, {(1, 1): c_both}, t, ((0, 1),), carry, outs)
    return projections, r_t.T


def solution(mesh):
    return jax.shard_map(
        functools.partial(per_device, dict(mesh.shape)),
        mesh=mesh,
        in_specs=(P("row", "col"), P("row", "col")),
        out_specs=(P("col", None), P("row", "col")),
        check_vma=False,
    )
```

```python
import functools

import jax
import jax.numpy as jnp
from jax import lax
from jax.experimental import pallas as pl
from jax.experimental.pallas import tpu as pltpu
from jax.sharding import PartitionSpec as P

F32, BF16 = jnp.float32, jnp.bfloat16
HIGHEST = lax.Precision.HIGHEST
NT, NN, TN = ((1,), (1,)), ((1,), (0,)), ((0,), (0,))
LANES, NB = 128, 64
VMEM_LIMIT = 16 * 2**20


def dot(a, b, dims, precision=None):
    return lax.dot_general(a, b, (dims, ((), ())), precision=precision, preferred_element_type=F32)


def split(x):
    hi = x.astype(BF16)
    return hi, (x - hi.astype(F32)).astype(BF16)


def params():
    return pltpu.CompilerParams(vmem_limit_bytes=VMEM_LIMIT)


def cost():
    return None


VM = pl.BlockSpec(memory_space=pltpu.VMEM)
HBM = pl.BlockSpec(memory_space=pltpu.HBM)
SMEM = pl.BlockSpec(memory_space=pltpu.SMEM)


def block_rows(m):
    for b in (752, 376):
        if m % b == 0:
            return b
    return m


Z, ODD, FIRST, OTHER, SIDE = 0, 1, 2, 3, 4


def touch_kernel(at_ref, p_ref, t_ref, o_ref, p_out, zero_ref):
    for i in range(at_ref.shape[0]):
        o_ref[i] = at_ref[i]
    p_out[...] = p_ref[...]
    zero_ref[...] = jnp.zeros_like(zero_ref)


def touch(at, p_t, t):
    return pl.pallas_call(
        touch_kernel,
        out_shape=[jax.ShapeDtypeStruct(s, d) for s, d in ((at.shape, jnp.int32), (p_t.shape, F32), (p_t.shape, F32))],
        in_specs=[SMEM, VM, VM],
        out_specs=[SMEM, VM, VM],
        compiler_params=params(),
        cost_estimate=cost(),
        name="touch",
    )(at, p_t, t)


def cross_kernel(at_ref, pa_ref, pb_ref, t_ref, *c_refs, halves):
    n = 2 * pa_ref.shape[0]
    m = t_ref.shape[0] // 2
    b = block_rows(m)
    pa, pb = pa_ref[...], pb_ref[...]
    swap = at_ref[ODD] != 0
    p_hi, p_lo = split(jnp.concatenate([jnp.where(swap, pb, pa), jnp.where(swap, pa, pb)], axis=0))
    both = jnp.concatenate([p_hi, p_lo], axis=0)
    refs = list(c_refs)
    for own, pieces in halves:
        half = at_ref[SIDE] if own else 1 - at_ref[SIDE]
        base = pl.multiple_of(half * m, 8)
        outs, refs = refs[:pieces], refs[pieces:]
        piece = m // pieces
        for i in range(0, m, b):
            t_hi, t_lo = split(t_ref[pl.ds(base + i, b), :])
            c = dot(t_hi, both, NT)
            c = c[:, :n] + c[:, n:] + dot(t_lo, p_hi, NT)
            if pieces == 1:
                outs[0][i : i + b, :] = c
            else:
                for j in range(0, b, piece):
                    outs[(i + j) // piece][...] = c[j : j + piece]


def cross(at, halves, pa, pb, t):
    m, n = t.shape[0] // 2, 2 * pa.shape[0]
    shapes = [(m // pieces, n) for _, pieces in halves for _ in range(pieces)]
    return pl.pallas_call(
        functools.partial(cross_kernel, halves=halves),
        out_shape=[jax.ShapeDtypeStruct(s, F32) for s in shapes],
        in_specs=[SMEM, VM, VM, VM],
        out_specs=[VM] * len(shapes),
        compiler_params=params(),
        cost_estimate=cost(),
        name="cross",
    )(at, pa, pb, t)


def gram_kernel(at_ref, own, pair, far, across, p_full, g_ref):
    w = own.shape[0]
    z = at_ref[Z]
    for flip, block in enumerate((own, pair, far, across)):
        p_full[pl.ds(pl.multiple_of((z ^ flip) * w, 8), w), :] = block[...]
    p = p_full[...]
    g_ref[...] = dot(p, p, NT, HIGHEST)


def gram4(at, *blocks):
    w, k = blocks[0].shape
    return pl.pallas_call(
        gram_kernel,
        out_shape=[jax.ShapeDtypeStruct((4 * w, k), F32), jax.ShapeDtypeStruct((4 * w, 4 * w), F32)],
        in_specs=[SMEM] + [VM] * 4,
        out_specs=[VM] * 2,
        compiler_params=params(),
        cost_estimate=cost(),
        name="gram",
    )(at, *blocks)


def plain_gram_kernel(p_ref, g_ref):
    p = p_ref[...]
    g_ref[...] = dot(p, p, NT, HIGHEST)


def plain_gram(p_t):
    n = p_t.shape[0]
    return pl.pallas_call(
        plain_gram_kernel,
        out_shape=jax.ShapeDtypeStruct((n, n), F32),
        in_specs=[VM],
        out_specs=VM,
        compiler_params=params(),
        cost_estimate=cost(),
        name="gram",
    )(p_t)


def tile(x):
    return jnp.broadcast_to(x, (8, LANES))


def eliminate(rows):
    sub = lax.broadcasted_iota(jnp.int32, (8, LANES), 0)
    n = len(rows)
    scaled = []
    for g in range(n):
        cols = [[tile(rows[i][:, 8 * g + c : 8 * g + c + 1]) for i in range(g, n)] for c in range(8)]
        own = rows[g]
        pivots = jnp.ones((8, LANES), F32)
        factors, lines = [], []
        for c in range(8):
            pivot = tile(cols[c][0][c : c + 1, :])
            inv = 1.0 / pivot
            f = [x * inv for x in cols[c]]
            f[0] = jnp.where(sub > c, f[0], 0.0)
            pivots = jnp.where(sub == c, pivot, pivots)
            for later in range(c + 1, 8):
                e = tile(cols[later][0][c : c + 1, :])
                cols[later] = [x - y * e for x, y in zip(cols[later], f)]
            line = tile(own[c : c + 1, :])
            own = own - f[0] * line
            factors.append(f)
            lines.append(line)
        for i in range(g + 1, n):
            for c in range(8):
                rows[i] = rows[i] - factors[c][i - g] * lines[c]
        scaled.append(own * lax.rsqrt(pivots))
    return scaled


def factor_steps(s, right, steps):
    i0 = lax.broadcasted_iota(jnp.int32, (NB, NB), 0)
    i1 = lax.broadcasted_iota(jnp.int32, (NB, NB), 1)
    eye = (i0 == i1).astype(F32)
    xs = []
    for _ in range(steps):
        augmented = jnp.concatenate([s[:NB, :NB], eye], axis=1)
        rows = eliminate([augmented[8 * i : 8 * i + 8] for i in range(NB // 8)])
        inv = jnp.concatenate(rows, axis=0)[:, NB:]
        x = dot(inv, right[:NB, :], NN, HIGHEST)
        xs.append(x)
        if s.shape[0] > NB:
            u = dot(inv, s[:NB, NB:], NN, HIGHEST)
            s = s[NB:, NB:] - dot(u, u, TN, HIGHEST)
            right = right[NB:, :] - dot(u, x, TN, HIGHEST)
    return xs, s, right


def begin_kernel(g_ref, x_ref, s_ref, r_ref):
    n = g_ref.shape[0]
    j0 = lax.broadcasted_iota(jnp.int32, (n, n), 0)
    j1 = lax.broadcasted_iota(jnp.int32, (n, n), 1)
    xs, s_ref[...], r_ref[...] = factor_steps(g_ref[...], (j0 == j1).astype(F32), x_ref.shape[0] // NB)
    x_ref[...] = jnp.concatenate(xs, axis=0)


def begin(g):
    n = g.shape[0]
    shapes = [(n - NB, n), (NB, NB), (NB, n)]
    return pl.pallas_call(
        begin_kernel,
        out_shape=[jax.ShapeDtypeStruct(s, F32) for s in shapes],
        in_specs=[VM],
        out_specs=[VM] * 3,
        compiler_params=params(),
        cost_estimate=cost(),
        name="begin",
    )(g)


def finish_kernel(x_ref, s_ref, r_ref, p_ref, lh_ref, ll_ref, qh_ref, ql_ref):
    (x,), _, _ = factor_steps(s_ref[...], r_ref[...], 1)
    linv = jnp.concatenate([x_ref[...], x], axis=0)
    lh_ref[...], ll_ref[...] = split(linv)
    qh_ref[...], ql_ref[...] = split(dot(linv, p_ref[...], NN, HIGHEST))


def finish(x, s, r, p_t):
    n, k = p_t.shape
    return pl.pallas_call(
        finish_kernel,
        out_shape=[jax.ShapeDtypeStruct((n, n), BF16)] * 2 + [jax.ShapeDtypeStruct((n, k), BF16)] * 2,
        in_specs=[VM] * 4,
        out_specs=[VM] * 4,
        compiler_params=params(),
        cost_estimate=cost(),
        name="finish",
    )(x, s, r, p_t)


def quarter_start(at_ref, place, rows):
    core, chip = place
    side = at_ref[OTHER if core else SIDE + 1]
    return pl.multiple_of((at_ref[SIDE] ^ core) * (rows // 2) + (side ^ chip) * (rows // 4), 8)


def update_kernel(at_ref, lh_ref, ll_ref, qh_ref, ql_ref, *refs, places, carried, into, last):
    c_refs, refs = refs[: len(places)], refs[len(places) :]
    t_ref, refs = refs[0], refs[1:]
    carry, refs = (refs[:2], refs[2:]) if carried else ((), refs)
    outs = refs[into:]
    rows = t_ref.shape[0]
    copies = []
    if last:
        p_out, r_out, *outs = outs
        sems = refs[-1]
    if carried:
        m = carry[0].shape[0] // len(carried)
        for j, place in enumerate(carried):
            here, there = pl.ds(j * m, m), pl.ds(quarter_start(at_ref, place, rows), m)
            copies += [
                pltpu.make_async_copy(carry[0].at[here], p_out.at[there], sems.at[0, j]),
                pltpu.make_async_copy(carry[1].at[here], r_out.at[there], sems.at[1, j]),
            ]
        for c in copies:
            c.start()
    p_here, r_here = outs[:2]
    lh, ll, qh, ql = lh_ref[...], ll_ref[...], qh_ref[...], ql_ref[...]
    m = c_refs[0].shape[0]
    cuts = [0, m // 2, m - m // 4 // 8 * 8, m] if last and m % 16 == 0 else [0, m]
    for j, (c_ref, place) in enumerate(zip(c_refs, places)):
        start = quarter_start(at_ref, place, rows)
        for i, (low, high) in enumerate(zip(cuts, cuts[1:])):
            here, there = pl.ds(j * m + low, high - low), pl.ds(start + low, high - low)
            c_hi, c_lo = split(c_ref[low:high, :])
            p = dot(c_hi, lh, NT) + dot(c_lo, lh, NT) + dot(c_hi, ll, NT)
            p_here[here, :] = p
            p_hi, p_lo = split(p)
            r_here[here, :] = t_ref[there, :] - (dot(p_hi, qh, NN) + dot(p_lo, qh, NN) + dot(p_hi, ql, NN))
            if last:
                s = len(carried) + j * (len(cuts) - 1) + i
                copies += [
                    pltpu.make_async_copy(p_here.at[here], p_out.at[there], sems.at[0, s]),
                    pltpu.make_async_copy(r_here.at[here], r_out.at[there], sems.at[1, s]),
                ]
                for c in copies[-2:]:
                    c.start()
    for c in copies:
        c.wait()


def update(at, parts, pieces, t, carried=(), carry=(), into=(), last=True):
    n, k = parts[2].shape
    m = t.shape[0]
    h = sum(x.shape[0] for x in pieces.values())
    own = [((h, n), F32), ((h, k), F32)]
    if last:
        out = [jax.ShapeDtypeStruct((m, n), F32), jax.ShapeDtypeStruct((m, k), F32)]
        scratch = [pltpu.VMEM(*x) for x in own] + [pltpu.SemaphoreType.DMA((2, len(carried) + 3 * len(pieces)))]
    else:
        out, scratch = [jax.ShapeDtypeStruct(*x) for x in own], []
    inputs = [at, *parts, *pieces.values(), t, *carry]
    return pl.pallas_call(
        functools.partial(update_kernel, places=tuple(pieces), carried=carried, into=len(into), last=last),
        out_shape=out,
        in_specs=[SMEM] + [VM] * (len(inputs) - 1) + [HBM] * len(into),
        out_specs=[HBM if last else VM] * 2,
        scratch_shapes=scratch,
        input_output_aliases={len(inputs) + i: i for i in range(len(into))},
        compiler_params=params(),
        cost_estimate=cost(),
        name="update",
    )(*inputs, *into)


class Rows:
    def __init__(self, count):
        self.count = count
        bits = list(range(1, count.bit_length() - 1))
        self.stages = [(0, 0)] + list(zip(bits, bits[::-1]))

    def swap(self, x, stage):
        by_core = self.stages[stage]
        return lax.ppermute(x, "row", [(r, r ^ (1 << by_core[r & 1])) for r in range(self.count)])

    def place(self, nz):
        me, z = lax.axis_index("row"), lax.axis_index("col")

        def sides(r):
            return [jnp.where(r & 1 == 0, (r >> b0) & 1, (r >> b1) & 1) for b0, b1 in self.stages]

        own = sides(me)
        flags = [z, z & 1, z >> 1] if nz == 4 else [z, 0, 0]
        at = jnp.stack([jnp.asarray(x, jnp.int32) for x in flags + [sides(me ^ 1)[1]] + own])
        return at, [jnp.broadcast_to(s == 1, (1, LANES)) for s in [flags[2]] + own]


class Order:
    def __init__(self):
        self.last = None

    def gate(self, x):
        return x if self.last is None else lax.optimization_barrier((x, self.last))[0]

    def run(self, f, x, *args):
        out = f(self.gate(x), *args)
        self.last = out[0] if isinstance(out, (list, tuple)) else out
        return out


def pick(flag, x, y):
    flag = jnp.broadcast_to(flag[:, :1], x.shape)
    return jnp.where(flag, y, x), jnp.where(flag, x, y)


def per_device(shape, panel, trailing):
    rows = Rows(shape["row"])
    end = len(rows.stages) - 1
    nz = shape["col"]
    at, upper = rows.place(nz)
    p_first = panel.T
    panel, trailing, at, upper = lax.optimization_barrier((panel, trailing, at, upper))
    p_own, t = panel.T, trailing.T
    n = p_own.shape[0] * nz
    second, *upper = upper

    def halved(stage, x, *more):
        h = x.shape[0] // 2
        low, high = x[:h], x[h:]
        for y in more:
            low, high = low + y[:h], high + y[h:]
        return pick(upper[stage], low, high)

    def joined(stage, x, got):
        return jnp.concatenate(pick(upper[stage], x, got))

    o = Order()

    def send(x, stage):
        x = o.gate(x)
        o.last = x
        return rows.swap(x, stage)

    def add(x, y):
        return o.run(lambda x: x + y, x)

    def cut(stage, x, *more):
        return o.run(lambda x: halved(stage, x, *more), x)

    def put(stage, x, got):
        return o.run(lambda x: joined(stage, x, got), x)

    def columns(x, y):
        return o.run(lambda y: jnp.concatenate(pick(second, x, y), axis=1), y)

    if nz == 4:
        def flipped(x, flip):
            return lax.ppermute(x, "col", [(z, z ^ flip) for z in range(nz)])

        pair, far = flipped(p_first, 1), flipped(p_own, 2)
        at, p_own, zero = touch(at, p_own, t)
        far = far + zero
        across = flipped(far, 1)
        o.last = far
        *out_a, a = o.run(lambda x: cross(at, ((False, 4), (True, 1)), x, pair, t), p_own)
        rest = (far, across)
    else:
        p_full = lax.all_gather(p_own, "col", axis=0, tiled=True)
        near, rest = [[p_full[i * (n // 4) : (i + 1) * (n // 4)] for i in h] for h in ((0, 1), (2, 3))]
        out_a, a = cross(at, ((False, 1), (True, 1)), *near, t)
    if nz == 4:
        got_a = [rows.swap(x, 0) for x in out_a]
        o.last = (out_a[0], across)
        def cut_pieces(x):
            q = got_a[0].shape[0]
            x = [x[i * q : (i + 1) * q] + y for i, y in enumerate(got_a)]
            pairs = [pick(upper[1], low, high) for low, high in zip(x[:2], x[2:])]
            return [jnp.concatenate(z) for z in zip(*pairs)]

        a, out_a = o.run(cut_pieces, a)
        o.last = out_a
    else:
        a, out_a = cut(1, a, send(out_a, 0))
    got_a = send(out_a, 1)
    if nz == 4:
        p_full, g = o.run(lambda x: gram4(at, x, pair, far, across), p_own)
        o.last = g
    else:
        g = o.run(plain_gram, p_full)
    g, out = cut(0, g)
    got_g = send(out, 0)
    (out_b,) = o.run(lambda x: cross(at, ((False, 1),), x, rest[1], t), rest[0])
    g = add(g, got_g)
    got_g = send(g, 1)
    for s in range(2, end):
        a, out_a = cut(s, a, got_a)
        got_a = send(out_a, s)
    a = add(a, got_a)
    got_a = send(a, end)
    got_b = send(out_b, 0)
    (b,) = o.run(lambda x: cross(at, ((True, 1),), x, rest[1], t), rest[0])
    for s in range(2, end + 1):
        g = add(g, got_g)
        got_g = send(g, s)
    b, out_b = cut(1, b, got_b)
    got_b = send(out_b, 1)
    a = add(a, got_a)
    for s in range(end - 1, 1, -1):
        a = put(s, a, send(a, s))
    for s in range(2, end):
        b, out_b = cut(s, b, got_b)
        got_b = send(out_b, s)
    b = add(b, got_b)
    g = add(g, got_g)
    got_g = send(g, 0)
    got_b = send(b, end)
    a_chip = send(a, 1)
    g = put(0, g, got_g)
    x, s_left, r_left = o.run(begin, g)
    o.last = (x, a_chip)
    b = add(b, got_b)
    for s in range(end - 1, 1, -1):
        b = put(s, b, send(b, s))
    b_chip = send(b, 1)
    c = columns(a, b)
    c_core = send(c, 0)
    parts = o.run(lambda p: finish(x, s_left, r_left, p), p_full)
    outs = o.run(lambda x: update(at, parts, {(0, 0): c, (1, 0): x}, t), c_core)
    c_chip = columns(a_chip, b_chip)
    c_both = send(c_chip, 0)
    carry = o.run(lambda x: update(at, parts, {(0, 1): x}, t, last=False), c_chip)
    projections, r_t = update(at, parts, {(1, 1): c_both}, t, ((0, 1),), carry, outs)
    return projections, r_t.T


def solution(mesh):
    return jax.shard_map(
        functools.partial(per_device, dict(mesh.shape)),
        mesh=mesh,
        in_specs=(P("row", "col"), P("row", "col")),
        out_specs=(P("col", None), P("row", "col")),
        check_vma=False,
    )
```
